32 devices in a mesh: node: 8 (over z, x), feat: 4 (over y, core).
Axes of the slice: x: 2, y: 2, z: 4, core: 2. Of those that a mesh axis runs over, the one named last changes fastest.
Arguments:
- features: bfloat16 [768, 65536], P('feat', 'node'), may hold values from -6 to 6
- neighbors: int32 [4096, 25], P('node'), may hold values from 0 to 511
- degrees: int32 [4096], P('node'), may hold values from 1 to 25
- tile_src: int32 [32, 4], P('node'), may hold values from 0 to 63
- tile_count: int32 [32], P('node'), may hold values from 1 to 4
- w_self: bfloat16 [768, 1024], P('feat'), may hold values from -0.21875 to 0.21875
- w_neigh: bfloat16 [768, 1024], P('feat'), may hold values from -0.21875 to 0.21875
- out_bias: float32 [1024], replicated, may hold values from -3 to 3
- d_out: bfloat16 [4096, 1024], P(('node', 'feat')), may hold values from -6 to 6
Outputs:
- output: bfloat16 [4096, 1024], P(('node', 'feat'))
- grad_features: bfloat16 [768, 65536], P('feat', 'node')
- grad_neigh: float32 [768, 1024], P('feat', 'node')
The draws below stay inside these ranges and needn't reach their ends.
All inputs are finite; a program needn't handle non-finite values.
Results may differ from the reference program's by a relative error of at most 0.0054.
Values may be sent and summed in bfloat16 or wider, within the bound.
A program may use at most 128 MiB of HBM per device.

```python
import math
import jax
import jax.numpy as jnp
from jax import lax

D_IN = 768
HID = 1024
FAN = 25
BLOCK = 128
KT = 4
SRC_DEV = 8192
DSTS = 512
NDST = 4096
NSRC = 65536
N_NODE = 8


def place_ends(result, rng, smallest, high):
    index_at = [jax.random.randint(jax.random.fold_in(rng, axis), (), 0, length) for axis, length in enumerate(result.shape)]
    longest = result.shape.index(max(result.shape))
    neighbour = index_at[:longest] + [(index_at[longest] + 1) % result.shape[longest]] + index_at[longest + 1:]
    return result.at[tuple(index_at)].set(smallest).at[tuple(neighbour)].set(high)


def spiked(entries, key, source, target, blocks, factor):
    def block_of(dim):
        return (jnp.arange(entries.shape[dim]) // (entries.shape[dim] // blocks)).reshape((-1,) + (1,) * (entries.ndim - 1 - dim))

    first = jax.random.permutation(key, blocks)[block_of(target)]
    other_side = (block_of(target) + blocks // 2) % blocks
    return jnp.where((block_of(source) == first) | (block_of(source) == other_side), factor * entries, entries)


def shard_levels(own_key, shape, pieces, low, top_value):
    def one(dim, parts):
        draws = jax.random.uniform(jax.random.fold_in(jax.random.fold_in(own_key, 6), dim), (parts,), jnp.float32, low / len(pieces), top_value / len(pieces))
        return jnp.repeat(jnp.exp(draws), shape[dim] // parts).reshape((-1,) + (1,) * (len(shape) - dim - 1))

    gain = one(*pieces[0])
    for cut in pieces[1:]:
        gain = gain * one(*cut)
    return gain


def noise(stream_key, dims, deviation, most, pieces=(), kind=jnp.bfloat16):
    gain = shard_levels(stream_key, dims, pieces, -0.22, 0.18) if pieces else 1.0
    entries = jax.random.normal(stream_key, dims, jnp.float32) * deviation * gain
    return jnp.minimum(jnp.maximum(entries, -most), most).astype(kind)


def heavy_noise(key, shape, scale, bound, split, heavy, kind=jnp.bfloat16):
    result = scale * jax.random.normal(key, shape, jnp.float32)
    if split:
        result = result * shard_levels(key, shape, split, -0.22, 0.18)
    return jnp.clip(spiked(result, jax.random.fold_in(key, 3), *heavy), -bound, bound).astype(kind)


def setup_inputs(seed: int = 0) -> dict:
    keys = jax.random.split(jax.random.key(seed), 10)
    return {
        "features": noise(keys[0], (D_IN, NSRC), 1.0, 6.0, ((0, 4), (1, 8))),
        "neighbors": place_ends(jax.random.randint(keys[1], (NDST, FAN), 0, KT * BLOCK), jax.random.fold_in(keys[1], 1), 0, (KT * BLOCK) - 1).astype(jnp.int32),
        "degrees": place_ends(jax.random.randint(keys[2], (NDST,), 1, FAN + 1), jax.random.fold_in(keys[2], 1), 1, FAN).astype(jnp.int32),
        "tile_src": place_ends(jax.random.randint(keys[3], (NDST // BLOCK, KT), 0, SRC_DEV // BLOCK), jax.random.fold_in(keys[3], 1), 0, (SRC_DEV // BLOCK) - 1).astype(jnp.int32),
        "tile_count": place_ends(jax.random.randint(keys[4], (NDST // BLOCK,), 1, KT + 1), jax.random.fold_in(keys[4], 1), 1, KT).astype(jnp.int32),
        "w_self": noise(keys[5], (D_IN, HID), D_IN ** -0.5, 0.21875, ((0, 4),)),
        "w_neigh": noise(keys[6], (D_IN, HID), D_IN ** -0.5, 0.21875, ((0, 4),)),
        "out_bias": noise(keys[7], (HID,), 0.5, 3.0, (), jnp.float32),
        "d_out": heavy_noise(keys[8], (NDST, HID), 1.0, 6.0, ((0, 32),), (0, 1, 32, 2.75)),
    }


def tile_counts(neighbors, degrees, tile_count, blocks, block, slot_count):
    fan_width = neighbors.shape[1]
    row_count = neighbors.shape[0]
    position = jnp.arange(fan_width, dtype=jnp.int32)
    block_live = jnp.repeat(tile_count, block)
    live_mask = (position[None, :] < degrees[:, None]) & (neighbors // block < block_live[:, None])
    row_ids = jnp.broadcast_to(jnp.arange(row_count, dtype=jnp.int32)[:, None], neighbors.shape)
    tallies = jnp.zeros((row_count, slot_count), jnp.float32).at[row_ids, neighbors].add(live_mask.astype(jnp.float32))
    return tallies.astype(jnp.bfloat16).reshape(blocks, block, slot_count)

def dot_rows(left_cols, weights):
    return lax.dot_general(left_cols, weights, (((0,), (0,)), ((), ())), preferred_element_type=jnp.float32)

def dot_cols(weights, grad_pre):
    return lax.dot_general(weights, grad_pre, (((1,), (1,)), ((), ())), preferred_element_type=jnp.float32)

def shard_pass(features, neighbors, degrees, tile_src, tile_count, w_self, w_neigh, out_bias, d_out):
    feat_rows = features.shape[0]
    node_count = neighbors.shape[0]
    blocks = tile_src.shape[0]
    slot_count = KT * BLOCK
    counts = tile_counts(neighbors, degrees, tile_count, blocks, BLOCK, slot_count)
    picked = features.reshape(feat_rows, -1, BLOCK)[:, tile_src, :].reshape(feat_rows, blocks, slot_count)
    summed = jnp.einsum('dbk,bjk->dbj', picked.astype(jnp.float32), counts.astype(jnp.float32))
    inverse = 1.0 / degrees.astype(jnp.float32)
    aggregate = (summed.reshape(feat_rows, node_count) * inverse).astype(jnp.bfloat16)
    own_cols = features[:, :node_count]
    pre_act = dot_rows(own_cols, w_self) + dot_rows(aggregate, w_neigh) + out_bias
    output = jax.nn.gelu(pre_act).astype(jnp.bfloat16)
    grad_pre = jax.vjp(jax.nn.gelu, pre_act)[1](d_out.astype(jnp.float32))[0].astype(jnp.bfloat16)
    partial_value = jnp.dot(aggregate, grad_pre, preferred_element_type=jnp.float32)
    back_neigh = dot_cols(w_neigh, grad_pre).astype(jnp.bfloat16)
    back_self = dot_cols(w_self, grad_pre).astype(jnp.bfloat16)
    scaled = (back_neigh.astype(jnp.float32) * inverse).astype(jnp.bfloat16).reshape(feat_rows, blocks, BLOCK)
    spread = jnp.einsum('dbj,bjk->dbk', scaled.astype(jnp.float32), counts.astype(jnp.float32))
    by_block = spread.reshape(feat_rows, blocks * KT, BLOCK).transpose(1, 0, 2)
    pooled = jax.ops.segment_sum(by_block, tile_src.reshape(-1), num_segments=features.shape[1] // BLOCK)
    grad_cols = pooled.transpose(1, 0, 2).reshape(feat_rows, -1)
    grad_cols = grad_cols.at[:, :node_count].add(back_self.astype(jnp.float32)).astype(jnp.bfloat16)
    return (output, grad_cols, partial_value)

def reference(features, neighbors, degrees, tile_src, tile_count, w_self, w_neigh, out_bias, d_out):
    shard_blocks = DSTS // BLOCK
    stacked = (neighbors.reshape(N_NODE, DSTS, FAN), degrees.reshape(N_NODE, DSTS), tile_src.reshape(N_NODE, shard_blocks, KT), tile_count.reshape(N_NODE, shard_blocks), d_out.reshape(N_NODE, DSTS, HID), jnp.arange(N_NODE, dtype=jnp.int32))

    def one_shard(running, items):
        shard_nbrs, shard_degs, shard_tiles, shard_live, shard_dout, shard = items
        shard_feats = lax.dynamic_slice_in_dim(features, (shard * SRC_DEV).astype(jnp.int32), SRC_DEV, 1)
        output, grad_cols, partial_value = shard_pass(shard_feats, shard_nbrs, shard_degs, shard_tiles, shard_live, w_self, w_neigh, out_bias, shard_dout)
        return (running + partial_value, (output, grad_cols))
    summed, (outputs, grads) = lax.scan(one_shard, jnp.zeros((D_IN, HID), jnp.float32), stacked)
    output = outputs.reshape(NDST, HID)
    grad_features = grads.transpose(1, 0, 2).reshape(D_IN, NSRC)
    grad_neigh = summed / math.sqrt(NDST)
    return (output, grad_features, grad_neigh)
```

```python
import functools
import math

import jax
import jax.numpy as jnp
from jax import lax
from jax.experimental import pallas as pl
from jax.experimental.pallas import tpu as pltpu
from jax.sharding import PartitionSpec as P

BLOCK = 128
KT = 4


def tile_counts(neighbors, degrees, tile_count, blocks, block, slot_count):
    fan_width = neighbors.shape[1]
    position = jnp.arange(fan_width, dtype=jnp.int32)
    block_live = jnp.repeat(tile_count, block)
    live_mask = (position[None, :] < degrees[:, None]) & (neighbors // block < block_live[:, None])
    slot_ids = jnp.arange(slot_count, dtype=jnp.int32)
    matches = (neighbors[:, :, None] == slot_ids[None, None, :]) & live_mask[:, :, None]
    tallies = jnp.sum(matches.astype(jnp.int32), axis=1)
    return tallies.astype(jnp.bfloat16).reshape(blocks, block, slot_count)


def dot_rows(left_cols, weights):
    return lax.dot_general(
        left_cols, weights, (((0,), (0,)), ((), ())), preferred_element_type=jnp.float32
    )


def dot_cols(weights, grad_pre):
    return lax.dot_general(
        weights, grad_pre, (((1,), (1,)), ((), ())), preferred_element_type=jnp.float32
    )


def body(features, neighbors, degrees, tile_src, tile_count, w_self, w_neigh, out_bias, d_out):
    feat_rows, src_width = features.shape
    node_count = neighbors.shape[0]
    blocks = tile_src.shape[0]
    slot_count = KT * BLOCK
    counts = tile_counts(neighbors, degrees, tile_count, blocks, BLOCK, slot_count)
    picked = features.reshape(feat_rows, src_width // BLOCK, BLOCK)[:, tile_src, :].reshape(
        feat_rows, blocks, slot_count
    )
    summed = jnp.einsum("dbk,bjk->dbj", picked, counts, preferred_element_type=jnp.float32)
    inverse = 1.0 / degrees.astype(jnp.float32)
    aggregate = (summed.reshape(feat_rows, node_count) * inverse).astype(jnp.bfloat16)
    own_cols = features[:, :node_count]
    aggregate_rows, own_rows = (
        lax.all_to_all(aggregate, "feat", split_axis=1, concat_axis=0, tiled=True),
        lax.all_to_all(own_cols, "feat", split_axis=1, concat_axis=0, tiled=True),
    )
    full_self, full_neigh = (
        lax.all_gather(w_self, "feat", axis=0, tiled=True),
        lax.all_gather(w_neigh, "feat", axis=0, tiled=True),
    )
    pre_act = dot_rows(own_rows, full_self) + dot_rows(aggregate_rows, full_neigh) + out_bias
    output = jax.nn.gelu(pre_act).astype(jnp.bfloat16)
    grad_pre = jax.vjp(jax.nn.gelu, pre_act)[1](d_out.astype(jnp.float32))[0].astype(jnp.bfloat16)
    grad_scale = 1.0 / math.sqrt(node_count * lax.axis_size("node"))
    partial_value = (
        jnp.dot(aggregate_rows, grad_pre, preferred_element_type=jnp.float32) * grad_scale
    )
    back_neigh = dot_cols(full_neigh, grad_pre).astype(jnp.bfloat16)
    back_self = dot_cols(full_self, grad_pre).astype(jnp.bfloat16)
    reduced = lax.psum_scatter(partial_value, "feat", scatter_dimension=0, tiled=True)
    grad_neigh = lax.psum_scatter(reduced, "node", scatter_dimension=1, tiled=True)
    neigh_cols, self_cols = (
        lax.all_to_all(back_neigh, "feat", split_axis=0, concat_axis=1, tiled=True),
        lax.all_to_all(back_self, "feat", split_axis=0, concat_axis=1, tiled=True),
    )
    scaled = (
        (neigh_cols.astype(jnp.float32) * inverse)
        .astype(jnp.bfloat16)
        .reshape(feat_rows, blocks, BLOCK)
    )
    spread = jnp.einsum("dbj,bjk->dbk", scaled, counts, preferred_element_type=jnp.float32)
    by_block = spread.reshape(feat_rows, blocks * KT, BLOCK).transpose(1, 0, 2)
    pooled = jax.ops.segment_sum(by_block, tile_src.reshape(-1), num_segments=src_width // BLOCK)
    grad_cols = pooled.transpose(1, 0, 2).reshape(feat_rows, src_width)
    grad_cols = grad_cols.at[:, :node_count].add(self_cols.astype(jnp.float32)).astype(jnp.bfloat16)
    return (output, grad_cols, grad_neigh)

MESH = pl.DeviceIdType.MESH
F32 = jnp.float32
BF16 = jnp.bfloat16


def remote(src, dst, send_sem, recv_sem, device):
    return pltpu.make_async_remote_copy(
        src_ref=src, dst_ref=dst, send_sem=send_sem, recv_sem=recv_sem, device_id=device, device_id_type=MESH
    )


def gather_kernel(tile_src, tile_count, features, nbrs, degrees, x_rows, x_trans, counts, own_cols, picked, own_sem, tile_sem):
    rows = features.shape[0]
    blocks = tile_src.shape[0]
    own = blocks * BLOCK
    fan = nbrs.shape[1]
    own_copy = pltpu.make_async_copy(features.at[:, pl.ds(0, own)], own_cols, own_sem)
    own_copy.start()
    copies = []
    for b in range(blocks):
        for k in range(KT):
            start = pl.multiple_of(tile_src[b, k] * BLOCK, BLOCK)
            copies.append(
                pltpu.make_async_copy(
                    features.at[:, pl.ds(start, BLOCK)],
                    picked.at[b, :, pl.ds(k * BLOCK, BLOCK)],
                    tile_sem.at[b * KT + k],
                )
            )
            copies[-1].start()

    def count_tile(tile, carry):
        b, k = tile // KT, tile % KT
        nb = nbrs[b]
        slot = lax.broadcasted_iota(jnp.int32, nb.shape, 0)
        live = (slot < degrees[b]) & (nb < tile_count[b] * BLOCK)
        offset = jnp.where(live, nb - k * BLOCK, -1)
        ids = lax.broadcasted_iota(jnp.int32, (BLOCK, BLOCK), 0)
        total = jnp.zeros((BLOCK, BLOCK), F32)
        for j in range(fan):
            total = total + jnp.where(ids == offset[j:j + 1, :], 1.0, 0.0)
        counts[tile] = total.astype(BF16)
        return carry

    lax.fori_loop(0, blocks * KT, count_tile, 0)
    own_copy.wait()
    x_rows[pl.ds(0, rows), :] = own_cols[...]
    for copy in copies:
        copy.wait()
    for b in range(blocks):
        tally = counts[pl.ds(b * KT, KT)].reshape(KT * BLOCK, BLOCK)
        summed = jnp.dot(picked[b], tally, preferred_element_type=F32)
        inverse = 1.0 / degrees[b].astype(F32)
        x_rows[pl.ds(rows, rows), pl.ds(b * BLOCK, BLOCK)] = (summed * inverse).astype(BF16)
    x_trans[...] = x_rows[...].T


def place_kernel(position, spread, back_self, grad_cols):
    step = pl.program_id(0)
    per = grad_cols.shape[1] // BLOCK
    tiles = spread.shape[0]
    own = back_self.shape[1] // BLOCK

    def value(i):
        at = position[step * per + i]
        tile = spread[jnp.minimum(at, tiles - 1)]
        return jnp.where(at < tiles, tile, 0.0)

    @pl.when(step == 0)
    def _():
        for i in range(per):
            tile = value(i)
            if i < own:
                tile = tile + back_self[:, i * BLOCK:(i + 1) * BLOCK].astype(F32)
            grad_cols[:, i * BLOCK:(i + 1) * BLOCK] = tile.astype(BF16)

    @pl.when(step > 0)
    def _():
        for i in range(per):
            grad_cols[:, i * BLOCK:(i + 1) * BLOCK] = value(i).astype(BF16)


def layer_kernel(
    n_node, grad_scale,
    same, x_rows, x_trans, counts, degrees, w_self, w_neigh, bias, d_out,
    output, spread, back_self, grad_neigh,
    merged, weights, partial_sum, core_in, y_out, y_in, grads, back, node_out, node_in,
    core_send, core_recv, y_send, y_recv, gy_send, gy_recv, gc_send, gc_recv, fw_send, fw_recv,
    node_send, node_recv,
):
    node = lax.axis_index("node")
    feat = lax.axis_index("feat")
    y, core = feat // 2, feat % 2
    rows = w_self.shape[0]
    blocks = degrees.shape[0]
    tiles = blocks * KT
    n_chunks = n_node // 2
    hid = bias.shape[1]
    width = hid // n_chunks
    half = width // 2
    core_feat = y * 2 + (1 - core)
    y_feat = (1 - y) * 2 + core
    diag_feat = (1 - y) * 2 + (1 - core)
    core_dev = (node, core_feat)
    y_dev = (node, y_feat)

    barrier = pltpu.get_barrier_semaphore()
    pl.semaphore_signal(barrier, inc=1, device_id=core_dev, device_id_type=MESH)
    pl.semaphore_signal(barrier, inc=1, device_id=y_dev, device_id_type=MESH)
    for step in range(1, n_node):
        pl.semaphore_signal(barrier, inc=1, device_id=((node + step) % n_node, feat), device_id_type=MESH)

    own = blocks * BLOCK
    weights[pl.ds(0, rows), :] = w_self[...]
    weights[pl.ds(rows, rows), :] = w_neigh[...]

    pl.semaphore_wait(barrier, n_node + 1)

    def columns(step):
        chunk = (node // 2 + step + 1) % n_chunks
        return chunk, pl.ds(pl.multiple_of(chunk * width, width), width)

    def core_copy(step):
        return remote(
            partial_sum.at[step, :, 1 - core], core_in.at[step], core_send.at[step], core_recv.at[step], core_dev
        )

    def y_copy(step):
        return remote(y_out.at[step], y_in.at[step], y_send.at[step], y_recv.at[step], y_dev)

    def grad_y(step, slot):
        ref = grads.at[step, slot]
        return remote(ref, ref, gy_send.at[step], gy_recv.at[step], y_dev)

    def grad_core(step, slot):
        ref = grads.at[step, slot]
        return remote(ref, ref, gc_send.at[step], gc_recv.at[step], core_dev)

    def grad_forward(step, slot):
        ref = grads.at[step, slot]
        return remote(ref, ref, fw_send.at[step], fw_recv.at[step], core_dev)

    def node_copy(step, side, target, sender):
        return remote(
            node_out.at[step, side], node_in.at[sender], node_send.at[step, side], node_recv.at[sender],
            (target, feat),
        )

    def to_y(step):
        core_copy(step).wait_recv()
        y_out[step] = (partial_sum[step, 1 - y, core] + core_in[step, 1 - y]).astype(BF16)
        y_copy(step).start()

    for step in range(n_chunks):
        _, cols = columns(step)
        product = jnp.dot(x_trans[...], weights[:, cols], preferred_element_type=F32)
        partial_sum[step] = product.reshape(2, 2, BLOCK, width)
        core_copy(step).start()
        if step >= 1:
            to_y(step - 1)
    to_y(n_chunks - 1)

    def merge_tile(tile, carry):
        for b in range(blocks):
            total = jnp.zeros((BLOCK, BLOCK), F32)
            for k in range(KT):
                total = total + counts[b * KT + k].astype(F32) * same[tile, b * KT + k]
            merged[tile, :, pl.ds(b * BLOCK, BLOCK)] = total.astype(BF16)
        return carry

    lax.fori_loop(0, tiles, merge_tile, 0)

    def activate(step):
        _, cols = columns(step)
        y_copy(step).wait_recv()
        v = partial_sum[step, y, core] + core_in[step, y] + y_in[step].astype(F32) + bias[:, cols]
        root = math.sqrt(2.0 / math.pi)
        square = v * v
        bend = jnp.tanh(root * v * (1.0 + 0.044715 * square))
        rise = 0.5 * (1.0 + bend)
        output[:, cols] = (v * rise).astype(BF16)
        slope = rise + 0.5 * v * (1.0 - bend * bend) * (root * (1.0 + 3.0 * 0.044715 * square))
        grads[step, feat] = (d_out[:, cols].astype(F32) * slope).astype(BF16)
        grad_y(step, feat).start()
        grad_core(step, feat).start()

    def forward(step):
        grad_y(step, y_feat).wait_recv()
        grad_forward(step, y_feat).start()

    def backward(step):
        chunk, cols = columns(step)
        grad_core(step, core_feat).wait_recv()
        grad_forward(step, diag_feat).wait_recv()
        g = grads[step].reshape(blocks * BLOCK, width)
        part = jnp.dot(x_rows[pl.ds(rows, rows), :], g, preferred_element_type=F32)
        for side in range(2):
            piece = part[:, side * half:(side + 1) * half]
            node_out[step, side] = piece.astype(BF16)
            if step < n_chunks - 1:
                node_copy(step, side, chunk * 2 + side, node).start()
        if step == n_chunks - 1:
            other = 1 - node % 2
            node_copy(step, other, chunk * 2 + other, node).start()
            mine = (node % 2).astype(F32)
            grad_neigh[...] = part[:, half:] * mine + part[:, :half] * (1.0 - mine)
        term = lax.dot_general(weights[:, cols], g, (((1,), (1,)), ((), ())), preferred_element_type=F32)
        if step == 0:
            back[...] = term
        else:
            back[...] += term

    for step in range(n_chunks + 2):
        if step < n_chunks:
            activate(step)
        if 1 <= step <= n_chunks:
            forward(step - 1)
        if step >= 2:
            backward(step - 2)

    scaled = jnp.concatenate(
        [
            (
                back[pl.ds(rows, rows), pl.ds(b * BLOCK, BLOCK)].astype(BF16).astype(F32)
                * (1.0 / degrees[b].astype(F32))
            ).astype(BF16)
            for b in range(blocks)
        ],
        axis=1,
    )
    for pair in range(tiles // 2):
        both = merged[pl.ds(pair * 2, 2)].reshape(2 * BLOCK, own)
        result = lax.dot_general(scaled, both, (((1,), (1,)), ((), ())), preferred_element_type=F32)
        spread[pair * 2] = result[:, :BLOCK]
        spread[pair * 2 + 1] = result[:, BLOCK:]
    back_self[...] = back[pl.ds(0, rows), :].astype(BF16)

    total = grad_neigh[...]
    for step in range(1, n_node):
        sender = (node + step) % n_node
        node_copy(0, 0, sender, sender).wait_recv()
        total = total + node_in[sender].astype(F32)
    grad_neigh[...] = total * grad_scale

    for step in range(n_chunks):
        core_copy(step).wait_send()
        y_copy(step).wait_send()
        grad_y(step, feat).wait_send()
        grad_core(step, feat).wait_send()
        grad_forward(step, y_feat).wait_send()
        if step < n_chunks - 1:
            for side in range(2):
                node_copy(step, side, (node + 1) % n_node, node).wait_send()
    other = 1 - node % 2
    node_copy(n_chunks - 1, other, node - node % 2 + other, node).wait_send()


def kernel_body(n_node, features, neighbors, degrees, tile_src, tile_count, w_self, w_neigh, out_bias, d_out):
    rows, src_width = features.shape
    nodes = neighbors.shape[0]
    blocks = tile_src.shape[0]
    tiles = blocks * KT
    hid = out_bias.shape[0]
    n_chunks = n_node // 2
    width = hid // n_chunks
    half = width // 2
    src_blocks = src_width // BLOCK
    flat = tile_src.reshape(-1)
    match = flat[None, :] == jnp.arange(src_blocks, dtype=jnp.int32)[:, None]
    found = jnp.max(jnp.where(match, jnp.arange(tiles, dtype=jnp.int32)[None, :], -1), axis=1)
    position = jnp.where(found < 0, tiles, found)
    nbrs = neighbors.reshape(blocks, BLOCK, -1).transpose(0, 2, 1)
    same = (flat[:, None] == flat[None, :]).astype(F32)
    degrees = degrees.reshape(blocks, 1, BLOCK)
    smem = pl.BlockSpec(memory_space=pltpu.SMEM)
    vmem = pl.BlockSpec(memory_space=pltpu.VMEM)
    dma = pltpu.SemaphoreType.DMA
    x_rows, x_trans, counts = pl.pallas_call(
        gather_kernel,
        out_shape=(
            jax.ShapeDtypeStruct((2 * rows, nodes), BF16),
            jax.ShapeDtypeStruct((nodes, 2 * rows), BF16),
            jax.ShapeDtypeStruct((tiles, BLOCK, BLOCK), BF16),
        ),
        in_specs=[smem, smem, pl.BlockSpec(memory_space=pl.ANY), vmem, vmem],
        out_specs=(vmem,) * 3,
        scratch_shapes=[
            pltpu.VMEM((rows, nodes), BF16),
            pltpu.VMEM((blocks, rows, KT * BLOCK), BF16),
            dma,
            dma((tiles,)),
        ],
        compiler_params=pltpu.CompilerParams(vmem_limit_bytes=24 * 1024 * 1024),
    )(tile_src, tile_count, features, nbrs, degrees)
    output, spread, back_self, grad_neigh = pl.pallas_call(
        functools.partial(layer_kernel, n_node, 1.0 / math.sqrt(nodes * n_node)),
        out_shape=(
            jax.ShapeDtypeStruct(d_out.shape, BF16),
            jax.ShapeDtypeStruct((tiles, rows, BLOCK), F32),
            jax.ShapeDtypeStruct((rows, nodes), BF16),
            jax.ShapeDtypeStruct((rows, half), F32),
        ),
        in_specs=[smem] + [vmem] * 8,
        out_specs=(vmem,) * 4,
        scratch_shapes=[
            pltpu.VMEM((tiles, BLOCK, nodes), BF16),
            pltpu.VMEM((2 * rows, hid), BF16),
            pltpu.VMEM((n_chunks, 2, 2, BLOCK, width), F32),
            pltpu.VMEM((n_chunks, 2, BLOCK, width), F32),
            pltpu.VMEM((n_chunks, BLOCK, width), BF16),
            pltpu.VMEM((n_chunks, BLOCK, width), BF16),
            pltpu.VMEM((n_chunks, 4, BLOCK, width), BF16),
            pltpu.VMEM((2 * rows, nodes), F32),
            pltpu.VMEM((n_chunks, 2, rows, half), BF16),
            pltpu.VMEM((n_node, rows, half), BF16),
        ]
        + [dma((n_chunks,))] * 10
        + [dma((n_chunks, 2)), dma((n_node,))],
        compiler_params=pltpu.CompilerParams(
            collective_id=0, has_side_effects=True, vmem_limit_bytes=32 * 1024 * 1024
        ),
    )(same, x_rows, x_trans, counts, degrees, w_self, w_neigh, out_bias.reshape(1, hid), d_out)
    steps = 8
    grad_cols = pl.pallas_call(
        place_kernel,
        grid=(steps,),
        out_shape=jax.ShapeDtypeStruct(features.shape, BF16),
        in_specs=[smem, vmem, vmem],
        out_specs=pl.BlockSpec((rows, src_width // steps), lambda i: (0, i)),
        compiler_params=pltpu.CompilerParams(vmem_limit_bytes=16 * 1024 * 1024),
    )(position, spread, back_self)
    return (output, grad_cols, grad_neigh)


def fits_kernel(n_node, n_feat):
    return n_feat == 4 and n_node == 8


def solution(mesh):
    n_node, n_feat = mesh.shape["node"], mesh.shape["feat"]
    placed = (
        P("feat", "node"),
        P("node", None),
        P("node"),
        P("node", None),
        P("node"),
        P("feat", None),
        P("feat", None),
        P(),
        P(("node", "feat"), None),
    )
    return jax.shard_map(
        functools.partial(kernel_body, n_node) if fits_kernel(n_node, n_feat) else body,
        mesh=mesh,
        in_specs=placed,
        out_specs=(P(("node", "feat"), None), P("feat", "node"), P("feat", "node")),
        check_vma=False,
    )
```
